512 devices in a mesh: batch: 32 (over y, x, core), tensor: 16 (over z).
Axes of the slice: x: 4, y: 4, z: 16, core: 2. Of those that a mesh axis runs over, the one named last changes fastest.
Arguments:
- normed_inputs: bfloat16 [4, 1024, 8192], P(None, 'batch', 'tensor'), may hold values from -6 to 6
- queries: bfloat16 [4, 1024, 8192], P(None, 'batch', 'tensor'), may hold values from -160 to 160
- key_value_weight: bfloat16 [2, 1024, 8192], P(None, 'tensor'), may hold values from -0.0625 to 0.0625
- adapter_down_maps: bfloat16 [256, 8192, 128], P('batch', 'tensor'), may hold values from -0.0625 to 0.0625
- adapter_up_maps: bfloat16 [256, 1024, 128], P('batch', 'tensor'), may hold values from -0.75 to 0.75
- stored_key_rows: bfloat16 [1024, 1024, 128], P('batch', 'tensor'), may hold values from -4.5 to 4.5
- stored_value_rows: bfloat16 [1024, 1024, 128], P('batch', 'tensor'), may hold values from -6 to 6
- request_adapter: int32 [1024], P('batch'), may hold values from 0 to 255, as said below
- lengths: int32 [1024], P('batch'), may hold values from 2 to 128, as said below
- adapter_storage: int32 [256], replicated, may hold values from 0 to 255, as said below
Outputs:
- attention_out: bfloat16 [4, 1024, 8192], P(None, 'batch', 'tensor')
The draws below stay inside these ranges and needn't reach their ends.
Inputs may be any that keep to these rules, and one draw needn't show every extreme that they name: request_adapter[r] is an adapter; among the 32 rows of one batch group at most 16 distinct adapters occur (exactly 16 in some group, 11 or more in every group), no two of them with the same adapter_storage value divided by 8, and no adapter on more than 3 of the group's rows (exactly 3 in some group). A permutation: adapter a is stored in slot adapter_storage[a] % 8 of batch group adapter_storage[a] // 8. `lengths`: some row has exactly 128 cached positions.
All inputs are finite; a program needn't handle non-finite values.
Results may differ from the reference program's by a relative error of at most 0.012.
Values may be sent and summed in bfloat16 or wider, within the bound.
No kernel may reach another device: no remote copies, remote signals or barrier semaphores. Data moves between devices by JAX's collectives and lax.ppermute only.
A program may use at most 64 MiB of HBM per device.

```python
import math
import jax
import jax.numpy as jnp
from jax import lax

MODEL_WIDTH = 8192
KVH = 8
HD = 128
ADAPTER_RANK = 64
ADP_DEV = 8
ROWS_DEV = 32
CTX = 128
STEPS = 4
SPLIT = 2
KEY_VALUE_WIDTH = 1024
GROUP = 8
DPD = 64
ROWS = 1024
ADAPTER_COUNT = 256
USED = 16
FEWEST = 11


def shared_keys(key):
    return jnp.clip(jax.random.normal(key, (ROWS, KEY_VALUE_WIDTH, CTX), jnp.float32), -4.5, 4.5)


def draw_stored_key_rows(key, part):
    base_keys = shared_keys(key)
    return base_keys.astype(jnp.bfloat16)


def draw_queries(key, part):
    key = jax.random.fold_in(key, 11)
    noise_key = jax.random.fold_in(key, 0)
    return jnp.clip(2.0 * jax.random.normal(noise_key, (STEPS, ROWS, MODEL_WIDTH), jnp.float32), -9.0, 9.0).astype(jnp.bfloat16)


def routing(key):
    owner_count = ADAPTER_COUNT // ADP_DEV
    group_count = ROWS // ROWS_DEV
    keys = jax.random.split(key, 7)
    adapter_storage = jax.random.permutation(keys[0], ADAPTER_COUNT).astype(jnp.int32)
    inverse = jnp.argsort(adapter_storage).astype(jnp.int32)
    counts = jax.random.randint(keys[1], (group_count,), FEWEST, USED + 1)
    widest = jax.random.randint(keys[2], (), 0, group_count)
    narrowest = (widest + 1 + jax.random.randint(keys[3], (), 0, group_count - 1)) % group_count
    group_ids = jnp.arange(group_count)
    counts = jnp.where(group_ids == widest, USED, jnp.where(group_ids == narrowest, FEWEST, counts))
    owner_order = jax.vmap(lambda sub: jax.random.permutation(sub, owner_count))(jax.random.split(keys[4], group_count))
    slot_table = jax.random.randint(keys[5], (group_count, owner_count), 0, ADP_DEV)
    row_order = jax.vmap(lambda sub: jax.random.permutation(sub, ROWS_DEV))(jax.random.split(keys[6], group_count))
    local_choice = row_order % counts[:, None]
    chosen_owner = jnp.take_along_axis(owner_order, local_choice, axis=1)
    chosen_slot = jnp.take_along_axis(slot_table, chosen_owner, axis=1)
    request_adapter = inverse[(chosen_owner * ADP_DEV + chosen_slot).reshape(ROWS)]
    return (adapter_storage, request_adapter.astype(jnp.int32))


def draw_adapter_storage(key, part):
    adapter_storage, request_adapter = routing(key)
    return adapter_storage


def draw_request_adapter(key, part):
    adapter_storage, request_adapter = routing(key)
    return request_adapter


def draw_lengths(key, part):
    key = jax.random.fold_in(key, 23)
    length_key, longest_key = jax.random.split(key, 2)
    length_draw = jax.random.randint(length_key, (ROWS,), 2, CTX + 1)
    longest = jax.random.randint(longest_key, (), 0, ROWS)
    return jnp.where(jnp.arange(ROWS) == longest, CTX, length_draw).astype(jnp.int32)


def block_levels(rng, shape, cuts, low, largest):
    factor_of, own = 1.0, jax.random.fold_in(rng, 6)
    for axis_at, blocks in cuts:
        draws = jnp.exp(jax.random.uniform(jax.random.fold_in(own, axis_at), (blocks,), jnp.float32, low / len(cuts), largest / len(cuts)))
        factor_of = factor_of * jnp.repeat(draws, shape[axis_at] // blocks).reshape([-1 if axis == axis_at else 1 for axis in range(len(shape))])
    return factor_of


def centred(key, shape, spread, reach, shards=(), dtype=jnp.bfloat16):
    drawn = jax.random.normal(key, shape, jnp.float32) * spread
    if len(shards) > 0:
        drawn = block_levels(key, shape, shards, -0.22, 0.18) * drawn
    return jnp.clip(drawn, min=-reach, max=reach).astype(dtype)


def setup_inputs(seed: int = 0) -> dict:
    splits = jax.random.split(jax.random.key(seed), 11)
    normed_inputs = centred(splits[0], (STEPS, ROWS, MODEL_WIDTH), 1.0, 6.0, ((1, 32), (2, 16)))
    queries = draw_queries(jax.random.fold_in(splits[10], 71), 0)
    key_value_weight = centred(splits[2], (2, KEY_VALUE_WIDTH, MODEL_WIDTH), MODEL_WIDTH ** -0.5, 0.0625, ((1, 16),))
    adapter_down_maps = centred(splits[3], (ADAPTER_COUNT, MODEL_WIDTH, 2 * ADAPTER_RANK), MODEL_WIDTH ** -0.5, 0.0625, ((0, 32), (1, 16)))
    adapter_up_maps = centred(splits[4], (ADAPTER_COUNT, KEY_VALUE_WIDTH, 2 * ADAPTER_RANK), ADAPTER_RANK ** -0.5, 0.75, ((0, 32), (1, 16)))
    stored_key_rows = draw_stored_key_rows(jax.random.fold_in(splits[10], 71), 0)
    stored_value_rows = centred(splits[6], (ROWS, KEY_VALUE_WIDTH, CTX), 1.0, 6.0, ((0, 32), (1, 16)))
    request_adapter = draw_request_adapter(jax.random.fold_in(splits[10], 71), 0)
    lengths = draw_lengths(jax.random.fold_in(splits[10], 71), 0)
    adapter_storage = draw_adapter_storage(jax.random.fold_in(splits[10], 71), 0)
    return {"normed_inputs": normed_inputs, "queries": queries, "key_value_weight": key_value_weight, "adapter_down_maps": adapter_down_maps, "adapter_up_maps": adapter_up_maps, "stored_key_rows": stored_key_rows, "stored_value_rows": stored_value_rows, "request_adapter": request_adapter, "lengths": lengths, "adapter_storage": adapter_storage}


def reference(normed_inputs, queries, key_value_weight, adapter_down_maps, adapter_up_maps, stored_key_rows, stored_value_rows, request_adapter, lengths, adapter_storage):
    position = jnp.take(adapter_storage, request_adapter, axis=0).astype(jnp.int32)
    flat_rows = normed_inputs.reshape(STEPS * ROWS, MODEL_WIDTH)
    base_kv = jnp.dot(flat_rows, key_value_weight.reshape(2 * KEY_VALUE_WIDTH, MODEL_WIDTH).T, preferred_element_type=jnp.float32)
    base_kv = base_kv.reshape(STEPS, ROWS, 2, KEY_VALUE_WIDTH)

    def adapter_row(row_inputs):
        row_states, request_position = row_inputs
        lowering_block = lax.dynamic_index_in_dim(adapter_down_maps, request_position, 0, keepdims=False)
        raising_block = lax.dynamic_index_in_dim(adapter_up_maps, request_position, 0, keepdims=False)
        shrink = jnp.dot(row_states, lowering_block, preferred_element_type=jnp.float32)
        return jnp.einsum('svk,cvk->svc', shrink.reshape(STEPS, 2, ADAPTER_RANK), raising_block.reshape(KEY_VALUE_WIDTH, 2, ADAPTER_RANK).astype(jnp.float32))
    delta = lax.map(adapter_row, (jnp.transpose(normed_inputs, (1, 0, 2)), position))
    new_kv = (base_kv + jnp.transpose(delta, (1, 0, 2, 3))).astype(jnp.bfloat16)
    new_kv = lax.optimization_barrier(new_kv)
    scale = 1.0 / math.sqrt(HD)
    causal = (jnp.arange(STEPS)[None, :] <= jnp.arange(STEPS)[:, None]).reshape(STEPS, 1, 1, STEPS)

    def attend_row(row_inputs):
        row_queries, row_keys, row_values, row_new, length = row_inputs
        query_heads = row_queries.reshape(STEPS, SPLIT, KVH, GROUP, DPD).transpose(0, 2, 3, 1, 4)
        query_heads = query_heads.reshape(STEPS, KVH, GROUP, HD).astype(jnp.float32)
        key_block = row_keys.reshape(SPLIT, KVH, DPD, CTX).transpose(1, 0, 2, 3).reshape(KVH, HD, CTX).astype(jnp.float32)
        value_block = row_values.reshape(SPLIT, KVH, DPD, CTX).transpose(1, 0, 2, 3).reshape(KVH, HD, CTX).astype(jnp.float32)
        fresh_keys = row_new[:, 0].reshape(STEPS, SPLIT, KVH, DPD).transpose(0, 2, 1, 3).reshape(STEPS, KVH, HD).astype(jnp.float32)
        fresh_values = row_new[:, 1].reshape(STEPS, SPLIT, KVH, DPD).transpose(0, 2, 1, 3).reshape(STEPS, KVH, HD).astype(jnp.float32)
        scores = jnp.einsum('shgd,hdt->shgt', query_heads, key_block) * scale
        fresh_scores = jnp.einsum('shgd,jhd->shgj', query_heads, fresh_keys) * scale
        valid_cache = (jnp.arange(CTX) < length).reshape(1, 1, 1, CTX)
        scores = jnp.where(valid_cache, scores, -jnp.inf)
        fresh_scores = jnp.where(causal, fresh_scores, -jnp.inf)
        highest = jnp.maximum(lax.optimization_barrier(jnp.max(scores, axis=-1, keepdims=True)), lax.optimization_barrier(jnp.max(fresh_scores, axis=-1, keepdims=True)))
        cache_exp = jnp.exp(scores - highest)
        fresh_exp = jnp.exp(fresh_scores - highest)
        running = lax.optimization_barrier(jnp.sum(cache_exp, axis=-1, keepdims=True)) + lax.optimization_barrier(jnp.sum(fresh_exp, axis=-1, keepdims=True))
        cache_weights = lax.optimization_barrier((cache_exp / running).astype(jnp.bfloat16)).astype(jnp.float32)
        fresh_weights = lax.optimization_barrier((fresh_exp / running).astype(jnp.bfloat16)).astype(jnp.float32)
        mixed = jnp.einsum('shgt,hdt->shgd', cache_weights, value_block)
        mixed = mixed + jnp.einsum('shgj,jhd->shgd', fresh_weights, fresh_values)
        mixed = mixed.astype(jnp.bfloat16).reshape(STEPS, KVH, GROUP, SPLIT, DPD).transpose(0, 3, 1, 2, 4)
        return mixed.reshape(STEPS, MODEL_WIDTH)
    outputs = lax.map(attend_row, (jnp.transpose(queries, (1, 0, 2)), stored_key_rows, stored_value_rows, jnp.transpose(new_kv, (1, 0, 2, 3)), lengths))
    return jnp.transpose(outputs, (1, 0, 2))
```

```python
import functools
import math

import jax
import jax.numpy as jnp
from jax import lax
from jax.experimental import pallas as pl
from jax.experimental.pallas import tpu as pltpu
from jax.sharding import PartitionSpec as P

HD = 128
MOST_ROWS = 3
SLOT_ROWS = 16
BF16 = jnp.bfloat16
F16 = jnp.float16
F32 = jnp.float32
X_SCALE = 2.0**12
PART_SCALE = 2.0**8
TURN_FLOPS = 2**36
VMEM = pl.BlockSpec(memory_space=pltpu.VMEM)
SMEM = pl.BlockSpec(memory_space=pltpu.SMEM)
HBM = pl.BlockSpec(memory_space=pltpu.HBM)


def partner(value):
    size = lax.axis_size("tensor")
    return lax.ppermute(value, "tensor", [(i, i ^ (size // 2)) for i in range(size)])


def pack(scores):
    steps = jnp.clip(jnp.round(scores * 2.0**11), -(2.0**23), 2.0**23 - 1).astype(jnp.int32)
    a, b, c, d = jnp.split(steps, 4, axis=0)
    low = 2**24 - 1
    return jnp.concatenate(
        [
            (a & low) | (d << 24),
            (b & low) | ((d >> 8) << 24),
            (c & low) | ((d >> 16) << 24),
        ],
        axis=0,
    )


def iota(shape, axis):
    return lax.broadcasted_iota(jnp.int32, shape, axis)


def dot(a, b, axes=((1,), (0,))):
    return lax.dot_general(a, b, (axes, ((), ())), preferred_element_type=F32)


def route_kernel(steps, rows, stored, *refs):
    adapter_in, storage_in, x_in, sent_ref, target_ref = refs[:5]
    counts, adapter_ref, storage_ref, x_ref, sems = refs[5:]
    copies = [
        pltpu.make_async_copy(source, here, sems.at[i])
        for i, (source, here) in enumerate(
            [(adapter_in, adapter_ref), (storage_in, storage_ref), (x_in, x_ref)]
        )
    ]
    for copy in copies:
        copy.start()
    groups, tokens = counts.shape[0], steps * rows
    for o in range(groups):
        counts[o] = 0
    copies[0].wait()
    copies[1].wait()
    lane = iota((1, tokens), 1)
    row_of = lane % rows
    target = jnp.zeros((1, tokens), jnp.int32)
    slots = jnp.zeros((1, tokens), jnp.int32)
    for r in range(rows):
        position = storage_ref[adapter_ref[r]]
        owner = position // stored
        place = counts[owner]
        counts[owner] = place + 1
        target = jnp.where(row_of == r, owner * SLOT_ROWS + place * steps, target)
        slots = jnp.where(row_of == r, position - owner * stored, slots)
    first = (target % SLOT_ROWS == 0) & (lane < rows)
    note_at = jnp.where(first, target + MOST_ROWS * steps, -1)
    target = target + lane // rows
    at = iota((groups * SLOT_ROWS, tokens), 0)
    pick = jnp.where(at == target, 1.0, 0.0).astype(BF16)
    note = jnp.sum(jnp.where(at == note_at, slots.astype(F32), 0.0), axis=1, keepdims=True)
    copies[2].wait()
    sent_ref[...] = (dot(pick, x_ref[...]) + note).astype(BF16)
    target_ref[...] = jnp.transpose(jnp.broadcast_to(target.astype(F32), (tokens, tokens))).astype(
        jnp.int32
    )


def turn_kernel(up_ref, out_ref):
    stored, cols, ranks = up_ref.shape
    for a in range(stored):
        turned = jnp.transpose(up_ref[a].astype(F32)).astype(BF16)
        out_ref[a] = jnp.concatenate([turned[: ranks // 2], turned[ranks // 2 :]], axis=1)


def owner_kernel(note_row, taken_ref, down_ref, up_ref, back_ref):
    stored, _, ranks = down_ref.shape
    groups = back_ref.shape[0]
    up_rows = up_ref.shape[1]
    taken = taken_ref[...]
    slot = taken.reshape(groups, SLOT_ROWS, -1)[:, note_row : note_row + 1, 0:1].astype(F32)
    for a in range(0, stored, 2):
        pair = dot(taken, jnp.concatenate([down_ref[a], down_ref[a + 1]], axis=1))
        for i in range(2):
            y = pair[:, i * ranks : (i + 1) * ranks].reshape(groups, SLOT_ROWS, ranks)
            lowered = y if a + i == 0 else jnp.where(slot == a + i, y, lowered)
    back_ref[:, up_rows:, :] = lowered.astype(BF16)
    for g in range(groups):
        mine = slot[g]
        chosen = up_ref[0].astype(F32)
        for a in range(1, stored):
            chosen = jnp.where(mine == a, up_ref[a].astype(F32), chosen)
        back_ref[g, :up_rows, :] = chosen.astype(BF16)


def scale_kernel(x_ref, out_ref):
    out_ref[...] = (x_ref[...].astype(F32) * X_SCALE).astype(BF16)


def rows_kernel(back_ref, target_ref, x_ref, both_ref):
    groups, _, ranks = back_ref.shape
    tokens = target_ref.shape[0]
    held = back_ref[:, -SLOT_ROWS:, :].reshape(groups * SLOT_ROWS, ranks)
    target = target_ref[...]
    pick = jnp.concatenate(
        [
            jnp.where(iota((tokens, tokens), 1) + b * tokens == target, 1.0, 0.0).astype(BF16)
            for b in range(groups * SLOT_ROWS // tokens)
        ],
        axis=1,
    )
    width = x_ref.shape[1]
    both_ref[:, :width] = x_ref[...]
    both_ref[:, width:] = (dot(pick, held) * PART_SCALE).astype(BF16)


def new_kernel(both_ref, back_ref, target_ref, w_ref, key_ref, value_ref, total):
    devices, tokens, _ = both_ref.shape
    groups, _, ranks = back_ref.shape
    width = both_ref.shape[2] - ranks
    half = ranks // 2
    shrink = both_ref[0, :, width:].astype(F32)
    for t in range(1, devices):
        shrink = shrink + both_ref[t, :, width:].astype(F32)
    shrink = shrink * (1.0 / PART_SCALE)
    owner = target_ref[...] // SLOT_ROWS
    total[...] = jnp.zeros_like(total)
    lane = iota((half, ranks), 1)
    for o in range(0, groups, 2):
        left, right = [], []
        for i in (o, o + 1):
            left.append(jnp.where(owner == i, shrink, 0.0).astype(BF16))
            up = back_ref[i, :half, :].astype(F32)
            right.append(jnp.where(lane < half, up, 0.0).astype(BF16))
            right.append(jnp.where(lane < half, 0.0, up).astype(BF16))
        total[...] += dot(jnp.concatenate(left, axis=1), jnp.concatenate(right, axis=0))
    total[...] = total[...] * X_SCALE
    for t in range(devices):
        total[...] += dot(
            both_ref[t, :, :width], w_ref[:, t * width : (t + 1) * width], ((1,), (1,))
        )
    total[...] = total[...] * (1.0 / X_SCALE)
    cols = key_ref.shape[1]
    key_ref[...] = total[:, :cols].astype(BF16)
    value_ref[...] = total[:, cols:].astype(BF16)


def whole_kernel(lengths_ref, words_ref, scores_ref, _, out_ref):
    rows, queries, positions = scores_ref.shape
    quarter = rows // 4
    inside = iota((queries, positions), 1)
    for i in range(quarter):
        a, b, c = (words_ref[i + k * quarter] for k in range(3))
        d = ((a >> 24) & 255) | (((b >> 24) & 255) << 8) | ((c >> 24) << 16)
        for k, steps in enumerate(((a << 8) >> 8, (b << 8) >> 8, (c << 8) >> 8, d)):
            r = i + k * quarter
            score = scores_ref[r] + steps.astype(F32) * 2.0**-11
            out_ref[r] = jnp.where(inside < lengths_ref[r], score, -jnp.inf)


def local(
    normed_inputs,
    queries,
    key_value_weight,
    adapter_down_maps,
    adapter_up_maps,
    stored_key_rows,
    stored_value_rows,
    request_adapter,
    lengths,
    adapter_storage,
):
    steps, rows, width = normed_inputs.shape
    tokens = steps * rows
    stored, _, ranks = adapter_down_maps.shape
    cols = key_value_weight.shape[1]
    positions = stored_key_rows.shape[2]
    groups = lax.axis_size("batch")
    devices = lax.axis_size("tensor")
    members = width // cols
    rank = ranks // 2
    full = key_value_weight.shape[2]
    params = pltpu.CompilerParams(vmem_limit_bytes=32 * 2**20)

    x = normed_inputs.reshape(tokens, width)

    scale = 1.0 / math.sqrt(HD)
    query = jnp.transpose(queries.reshape(steps, rows, members, cols), (1, 0, 2, 3))
    query = query.reshape(rows, steps * members, cols)
    scores = scale * jnp.einsum(
        "rme,ret->rmt", query, stored_key_rows, preferred_element_type=F32
    )
    packed, x = lax.optimization_barrier((pack(scores), x))
    words = partner(packed)

    sent, target = pl.pallas_call(
        functools.partial(route_kernel, steps, rows, stored),
        out_shape=(
            jax.ShapeDtypeStruct((groups * SLOT_ROWS, width), BF16),
            jax.ShapeDtypeStruct((tokens, tokens), jnp.int32),
        ),
        in_specs=[HBM] * 3,
        out_specs=(VMEM, VMEM),
        scratch_shapes=[
            pltpu.SMEM((groups,), jnp.int32),
            pltpu.SMEM(request_adapter.shape, jnp.int32),
            pltpu.SMEM(adapter_storage.shape, jnp.int32),
            pltpu.VMEM(x.shape, BF16),
            pltpu.SemaphoreType.DMA((3,)),
        ],
        compiler_params=pltpu.CompilerParams(vmem_limit_bytes=60 * 2**20),
        name="route",
    )(request_adapter, adapter_storage, x)
    taken = lax.all_to_all(
        sent.reshape(groups, SLOT_ROWS, width), "batch", 0, 0, tiled=True
    ).reshape(groups * SLOT_ROWS, width)
    up = pl.pallas_call(
        turn_kernel,
        out_shape=jax.ShapeDtypeStruct((stored, rank, 2 * cols), BF16),
        in_specs=[VMEM],
        out_specs=VMEM,
        compiler_params=params,
        cost_estimate=pl.CostEstimate(flops=TURN_FLOPS, bytes_accessed=2**18, transcendentals=0),
        name="turn",
    )(adapter_up_maps)
    back = pl.pallas_call(
        functools.partial(owner_kernel, MOST_ROWS * steps),
        out_shape=jax.ShapeDtypeStruct((groups, rank + SLOT_ROWS, ranks), BF16),
        in_specs=[VMEM] * 3,
        out_specs=VMEM,
        compiler_params=params,
        name="owner",
    )(taken, adapter_down_maps, up)
    back = lax.all_to_all(back, "batch", 0, 0, tiled=True)
    scaled = pl.pallas_call(
        scale_kernel,
        out_shape=jax.ShapeDtypeStruct(x.shape, BF16),
        in_specs=[VMEM],
        out_specs=VMEM,
        compiler_params=params,
        cost_estimate=pl.CostEstimate(flops=TURN_FLOPS, bytes_accessed=2**18, transcendentals=0),
        name="scale",
    )(x)
    both = pl.pallas_call(
        rows_kernel,
        out_shape=jax.ShapeDtypeStruct((tokens, width + ranks), BF16),
        in_specs=[VMEM] * 3,
        out_specs=VMEM,
        compiler_params=params,
        name="rows",
    )(back, target, scaled)
    both = lax.all_gather(both.astype(F16), "tensor", axis=0, tiled=False).astype(BF16)
    new_shape = jax.ShapeDtypeStruct((tokens, cols), BF16)
    fresh_keys, fresh_values = pl.pallas_call(
        new_kernel,
        out_shape=(new_shape, new_shape),
        in_specs=[VMEM] * 4,
        out_specs=(VMEM, VMEM),
        scratch_shapes=[pltpu.VMEM((tokens, 2 * cols), F32)],
        compiler_params=params,
        name="new_kv",
    )(both, back, target, key_value_weight.reshape(2 * cols, full))
    fresh_keys = fresh_keys.reshape(steps, rows, cols)
    fresh_values = fresh_values.reshape(steps, rows, cols)

    fresh = jnp.einsum("rme,jre->rjm", query, fresh_keys, preferred_element_type=F32)
    fresh = fresh.reshape(rows, -1)
    scores = pl.pallas_call(
        whole_kernel,
        out_shape=jax.ShapeDtypeStruct(scores.shape, F32),
        in_specs=[SMEM, VMEM, VMEM, HBM],
        out_specs=VMEM,
        compiler_params=params,
        name="whole",
    )(lengths, words, scores, fresh)
    peak = jnp.max(scores, axis=-1)
    risen = jnp.exp(scores - peak[:, :, None])
    mass = jnp.sum(risen, axis=-1)
    cached = jnp.einsum(
        "rmt,ret->rme", risen.astype(BF16), stored_value_rows, preferred_element_type=F32
    )
    fresh = (fresh + partner(fresh)).reshape(rows, steps, -1)
    step_of = jnp.arange(steps * members) // members
    causal = (jnp.arange(steps)[:, None] <= step_of[None, :])[None]
    fresh = jnp.where(causal, fresh * scale, -jnp.inf)
    highest = jnp.maximum(peak, jnp.max(fresh, axis=1))
    fresh_exp = jnp.exp(fresh - highest[:, None, :])
    fall = jnp.exp(peak - highest)
    sums = mass * fall + jnp.sum(fresh_exp, axis=1)
    fresh_weights = (fresh_exp / sums[:, None, :]).astype(BF16)
    mixed = cached * (fall / sums)[:, :, None] + jnp.einsum(
        "rjm,jre->rme", fresh_weights, fresh_values, preferred_element_type=F32
    )
    mixed = mixed.astype(BF16).reshape(rows, steps, members * cols)
    return jnp.transpose(mixed, (1, 0, 2))


def solution(mesh):
    return jax.shard_map(
        local,
        mesh=mesh,
        in_specs=(
            P(None, "batch", "tensor"),
            P(None, "batch", "tensor"),
            P(None, "tensor", None),
            P("batch", "tensor", None),
            P("batch", "tensor", None),
            P("batch", "tensor", None),
            P("batch", "tensor", None),
            P("batch"),
            P("batch"),
            P(),
        ),
        out_specs=P(None, "batch", "tensor"),
        check_vma=False,
    )
```

```python
import functools
import math

import jax
import jax.numpy as jnp
from jax import lax
from jax.experimental import pallas as pl
from jax.experimental.pallas import tpu as pltpu
from jax.sharding import PartitionSpec as P

HD = 128
MOST_ROWS = 3
SLOT_ROWS = 16
BF16 = jnp.bfloat16
F16 = jnp.float16
F32 = jnp.float32
X_SCALE = 2.0**12
PART_SCALE = 2.0**8
TURN_FLOPS = 2**36
VMEM = pl.BlockSpec(memory_space=pltpu.VMEM)
SMEM = pl.BlockSpec(memory_space=pltpu.SMEM)
HBM = pl.BlockSpec(memory_space=pltpu.HBM)


def partner(value):
    size = lax.axis_size("tensor")
    return lax.ppermute(value, "tensor", [(i, i ^ (size // 2)) for i in range(size)])


def pack(scores):
    steps = jnp.clip(jnp.round(scores * 2.0**11), -(2.0**23), 2.0**23 - 1).astype(jnp.int32)
    a, b, c, d = jnp.split(steps, 4, axis=0)
    low = 2**24 - 1
    return jnp.concatenate(
        [
            (a & low) | (d << 24),
            (b & low) | ((d >> 8) << 24),
            (c & low) | ((d >> 16) << 24),
        ],
        axis=0,
    )


def iota(shape, axis):
    return lax.broadcasted_iota(jnp.int32, shape, axis)


def dot(a, b, axes=((1,), (0,))):
    return lax.dot_general(a, b, (axes, ((), ())), preferred_element_type=F32)


def route_kernel(steps, rows, stored, adapter_ref, storage_ref, x_ref, sent_ref, target_ref):
    tokens = steps * rows
    count = storage_ref.shape[1]
    groups = count // stored
    adapter = jnp.concatenate([adapter_ref[...]] * steps, axis=1)
    hits = jnp.where(iota((count, tokens), 0) == adapter, 1.0, 0.0).astype(BF16)
    storage = jnp.broadcast_to(storage_ref[...].astype(F32), (8, count)).astype(BF16)
    position = dot(storage, hits)[0:1]
    down = jnp.transpose(jnp.broadcast_to(position, (tokens, tokens))).astype(jnp.int32)
    position = position.astype(jnp.int32)
    owner = position // stored
    earlier = iota((rows, tokens), 0) < iota((rows, tokens), 1) % rows
    same = earlier & (down[:rows] // stored == owner)
    place = jnp.sum(jnp.where(same, 1.0, 0.0), axis=0, keepdims=True).astype(jnp.int32)
    lane = iota((1, tokens), 1)
    target = owner * SLOT_ROWS + place * steps + lane // rows
    noted = jnp.where((place == 0) & (lane < rows), owner * SLOT_ROWS + MOST_ROWS * steps, -1)
    at = iota((groups * SLOT_ROWS, tokens), 0)
    pick = jnp.concatenate(
        [jnp.where(at == t, 1.0, 0.0).astype(BF16) for t in (target, noted)], axis=1
    )
    slot = (down % stored).astype(F32).astype(BF16)
    slot = jnp.concatenate([slot] * (x_ref.shape[1] // tokens), axis=1)
    sent_ref[...] = dot(pick, jnp.concatenate([x_ref[...], slot], axis=0)).astype(BF16)
    target_ref[...] = jnp.broadcast_to(target, target_ref.shape)


def turn_kernel(up_ref, target_ref, out_ref, turned_ref):
    stored, cols, ranks = up_ref.shape
    for a in range(stored):
        turned = jnp.transpose(up_ref[a].astype(F32)).astype(BF16)
        out_ref[a] = jnp.concatenate([turned[: ranks // 2], turned[ranks // 2 :]], axis=1)
    tokens = target_ref.shape[1]
    target = jnp.broadcast_to(target_ref[0:1].astype(F32), (tokens, tokens))
    turned_ref[...] = jnp.transpose(target).astype(jnp.int32)


def owner_kernel(note_row, taken_ref, down_ref, up_ref, back_ref):
    stored, _, ranks = down_ref.shape
    groups = back_ref.shape[0]
    up_rows = up_ref.shape[1]
    taken = taken_ref[...]
    slot = taken.reshape(groups, SLOT_ROWS, -1)[:, note_row : note_row + 1, 0:1].astype(F32)
    for a in range(0, stored, 2):
        pair = dot(taken, jnp.concatenate([down_ref[a], down_ref[a + 1]], axis=1))
        for i in range(2):
            y = pair[:, i * ranks : (i + 1) * ranks].reshape(groups, SLOT_ROWS, ranks)
            lowered = y if a + i == 0 else jnp.where(slot == a + i, y, lowered)
    back_ref[:, up_rows:, :] = lowered.astype(BF16)
    maps = [up_ref[a].astype(F32) for a in range(stored)]
    for g in range(groups):
        mine = slot[g]
        chosen = maps[0]
        for a in range(1, stored):
            chosen = jnp.where(mine == a, maps[a], chosen)
        back_ref[g, :up_rows, :] = chosen.astype(BF16)


def scale_kernel(x_ref, out_ref):
    out_ref[...] = (x_ref[...].astype(F32) * X_SCALE).astype(BF16)


def rows_kernel(back_ref, target_ref, x_ref, both_ref):
    groups, _, ranks = back_ref.shape
    tokens = target_ref.shape[0]
    held = back_ref[:, -SLOT_ROWS:, :].reshape(groups * SLOT_ROWS, ranks)
    target = target_ref[...]
    pick = jnp.concatenate(
        [
            jnp.where(iota((tokens, tokens), 1) + b * tokens == target, 1.0, 0.0).astype(BF16)
            for b in range(groups * SLOT_ROWS // tokens)
        ],
        axis=1,
    )
    width = x_ref.shape[1]
    both_ref[:, :width] = x_ref[...]
    both_ref[:, width:] = (dot(pick, held) * PART_SCALE).astype(BF16)


def delta_kernel(both_ref, back_ref, target_ref, out_ref):
    devices, tokens, _ = both_ref.shape
    groups, _, ranks = back_ref.shape
    width = both_ref.shape[2] - ranks
    half = ranks // 2
    shrink = both_ref[0, :, width:].astype(F32)
    for t in range(1, devices):
        shrink = shrink + both_ref[t, :, width:].astype(F32)
    shrink = shrink * (1.0 / PART_SCALE)
    owner = target_ref[...] // SLOT_ROWS
    lane = iota((half, ranks), 1)
    out_ref[...] = jnp.zeros_like(out_ref)
    for o in range(0, groups, 2):
        left, right = [], []
        for i in (o, o + 1):
            left.append(jnp.where(owner == i, shrink, 0.0).astype(BF16))
            up = back_ref[i, :half, :].astype(F32)
            right.append(jnp.where(lane < half, up, 0.0).astype(BF16))
            right.append(jnp.where(lane < half, 0.0, up).astype(BF16))
        out_ref[...] += dot(jnp.concatenate(left, axis=1), jnp.concatenate(right, axis=0))


def new_kernel(both_ref, delta_ref, w_ref, key_ref, value_ref, total):
    cols = key_ref.shape[1]
    devices = both_ref.shape[0]
    width = w_ref.shape[1] // devices
    total[...] = delta_ref[...] * X_SCALE
    for t in range(devices):
        total[...] += dot(
            both_ref[t, :, :width], w_ref[:, t * width : (t + 1) * width], ((1,), (1,))
        )
    new = (total[...] * (1.0 / X_SCALE)).astype(BF16)
    key_ref[...] = new[:, :cols]
    value_ref[...] = new[:, cols:]


def whole_kernel(lengths_ref, words_ref, scores_ref, _, out_ref):
    rows, queries, positions = scores_ref.shape
    quarter = rows // 4
    inside = iota((queries, positions), 1)
    for i in range(quarter):
        a, b, c = (words_ref[i + k * quarter] for k in range(3))
        d = ((a >> 24) & 255) | (((b >> 24) & 255) << 8) | ((c >> 24) << 16)
        for k, steps in enumerate(((a << 8) >> 8, (b << 8) >> 8, (c << 8) >> 8, d)):
            r = i + k * quarter
            score = scores_ref[r] + steps.astype(F32) * 2.0**-11
            out_ref[r] = jnp.where(inside < lengths_ref[r], score, -jnp.inf)


def local(
    normed_inputs,
    queries,
    key_value_weight,
    adapter_down_maps,
    adapter_up_maps,
    stored_key_rows,
    stored_value_rows,
    request_adapter,
    lengths,
    adapter_storage,
):
    steps, rows, width = normed_inputs.shape
    tokens = steps * rows
    stored, _, ranks = adapter_down_maps.shape
    cols = key_value_weight.shape[1]
    positions = stored_key_rows.shape[2]
    groups = lax.axis_size("batch")
    devices = lax.axis_size("tensor")
    members = width // cols
    rank = ranks // 2
    full = key_value_weight.shape[2]
    params = pltpu.CompilerParams(vmem_limit_bytes=32 * 2**20)

    x = normed_inputs.reshape(tokens, width)

    scale = 1.0 / math.sqrt(HD)
    query = jnp.transpose(queries.reshape(steps, rows, members, cols), (1, 0, 2, 3))
    query = query.reshape(rows, steps * members, cols)
    scores = scale * jnp.einsum(
        "rme,ret->rmt", query, stored_key_rows, preferred_element_type=F32
    )
    packed, x = lax.optimization_barrier((pack(scores), x))
    words = partner(packed)

    sent, target = pl.pallas_call(
        functools.partial(route_kernel, steps, rows, stored),
        out_shape=(
            jax.ShapeDtypeStruct((groups * SLOT_ROWS, width), BF16),
            jax.ShapeDtypeStruct((8, tokens), jnp.int32),
        ),
        in_specs=[VMEM] * 3,
        out_specs=(VMEM, VMEM),
        compiler_params=params,
        name="route",
    )(request_adapter.reshape(1, -1), adapter_storage.reshape(1, -1), x)
    taken = lax.all_to_all(
        sent.reshape(groups, SLOT_ROWS, width), "batch", 0, 0, tiled=True
    ).reshape(groups * SLOT_ROWS, width)
    up, target = pl.pallas_call(
        turn_kernel,
        out_shape=(
            jax.ShapeDtypeStruct((stored, rank, 2 * cols), BF16),
            jax.ShapeDtypeStruct((tokens, tokens), jnp.int32),
        ),
        in_specs=[VMEM] * 2,
        out_specs=(VMEM, VMEM),
        compiler_params=params,
        cost_estimate=pl.CostEstimate(flops=TURN_FLOPS, bytes_accessed=2**18, transcendentals=0),
        name="turn",
    )(adapter_up_maps, target)
    back = pl.pallas_call(
        functools.partial(owner_kernel, MOST_ROWS * steps),
        out_shape=jax.ShapeDtypeStruct((groups, rank + SLOT_ROWS, ranks), BF16),
        in_specs=[VMEM] * 3,
        out_specs=VMEM,
        compiler_params=params,
        name="owner",
    )(taken, adapter_down_maps, up)
    back = lax.all_to_all(back, "batch", 0, 0, tiled=True)
    scaled = pl.pallas_call(
        scale_kernel,
        out_shape=jax.ShapeDtypeStruct(x.shape, BF16),
        in_specs=[VMEM],
        out_specs=VMEM,
        compiler_params=params,
        cost_estimate=pl.CostEstimate(flops=TURN_FLOPS, bytes_accessed=2**18, transcendentals=0),
        name="scale",
    )(x)
    both = pl.pallas_call(
        rows_kernel,
        out_shape=jax.ShapeDtypeStruct((tokens, width + ranks), BF16),
        in_specs=[VMEM] * 3,
        out_specs=VMEM,
        compiler_params=params,
        name="rows",
    )(back, target, scaled)
    both = lax.all_gather(both.astype(F16), "tensor", axis=0, tiled=False).astype(BF16)
    delta = pl.pallas_call(
        delta_kernel,
        out_shape=jax.ShapeDtypeStruct((tokens, 2 * cols), F32),
        in_specs=[VMEM] * 3,
        out_specs=VMEM,
        compiler_params=params,
        name="delta",
    )(both, back, target)
    new_shape = jax.ShapeDtypeStruct((tokens, cols), BF16)
    fresh_keys, fresh_values = pl.pallas_call(
        new_kernel,
        out_shape=(new_shape, new_shape),
        in_specs=[VMEM] * 3,
        out_specs=(VMEM, VMEM),
        scratch_shapes=[pltpu.VMEM((tokens, 2 * cols), F32)],
        compiler_params=params,
        name="new_kv",
    )(both, delta, key_value_weight.reshape(2 * cols, full))
    fresh_keys = fresh_keys.reshape(steps, rows, cols)
    fresh_values = fresh_values.reshape(steps, rows, cols)

    fresh = jnp.einsum("rme,jre->rjm", query, fresh_keys, preferred_element_type=F32)
    fresh = fresh.reshape(rows, -1)
    scores = pl.pallas_call(
        whole_kernel,
        out_shape=jax.ShapeDtypeStruct(scores.shape, F32),
        in_specs=[SMEM, VMEM, VMEM, HBM],
        out_specs=VMEM,
        compiler_params=params,
        name="whole",
    )(lengths, words, scores, fresh)
    peak = jnp.max(scores, axis=-1)
    risen = jnp.exp(scores - peak[:, :, None])
    mass = jnp.sum(risen, axis=-1)
    cached = jnp.einsum(
        "rmt,ret->rme", risen.astype(BF16), stored_value_rows, preferred_element_type=F32
    )
    cached, peak, mass = lax.optimization_barrier((cached, peak, mass))
    fresh = (fresh + partner(fresh)).reshape(rows, steps, -1)
    step_of = jnp.arange(steps * members) // members
    causal = (jnp.arange(steps)[:, None] <= step_of[None, :])[None]
    fresh = jnp.where(causal, fresh * scale, -jnp.inf)
    highest = jnp.maximum(peak, jnp.max(fresh, axis=1))
    fresh_exp = jnp.exp(fresh - highest[:, None, :])
    fall = jnp.exp(peak - highest)
    sums = mass * fall + jnp.sum(fresh_exp, axis=1)
    fresh_weights = (fresh_exp / sums[:, None, :]).astype(BF16)
    mixed = cached * (fall / sums)[:, :, None] + jnp.einsum(
        "rjm,jre->rme", fresh_weights, fresh_values, preferred_element_type=F32
    )
    mixed = mixed.astype(BF16).reshape(rows, steps, members * cols)
    return jnp.transpose(mixed, (1, 0, 2))


def solution(mesh):
    return jax.shard_map(
        local,
        mesh=mesh,
        in_specs=(
            P(None, "batch", "tensor"),
            P(None, "batch", "tensor"),
            P(None, "tensor", None),
            P("batch", "tensor", None),
            P("batch", "tensor", None),
            P("batch", "tensor", None),
            P("batch", "tensor", None),
            P("batch"),
            P("batch"),
            P(),
        ),
        out_specs=P(None, "batch", "tensor"),
        check_vma=False,
    )
```

```python
import functools
import math

import jax
import jax.numpy as jnp
from jax import lax
from jax.experimental import pallas as pl
from jax.experimental.pallas import tpu as pltpu
from jax.sharding import PartitionSpec as P

HD = 128
MOST_ROWS = 3
SLOT_ROWS = 16
BF16 = jnp.bfloat16
F16 = jnp.float16
F32 = jnp.float32
X_SCALE = 2.0**12
PART_SCALE = 2.0**8
TURN_FLOPS = 2**36
VMEM = pl.BlockSpec(memory_space=pltpu.VMEM)
SMEM = pl.BlockSpec(memory_space=pltpu.SMEM)
HBM = pl.BlockSpec(memory_space=pltpu.HBM)


def partner(value):
    size = lax.axis_size("tensor")
    return lax.ppermute(value, "tensor", [(i, i ^ (size // 2)) for i in range(size)])


def pack(scores):
    steps = jnp.clip(jnp.round(scores * 2.0**11), -(2.0**23), 2.0**23 - 1).astype(jnp.int32)
    a, b, c, d = jnp.split(steps, 4, axis=0)
    low = 2**24 - 1
    return jnp.concatenate(
        [
            (a & low) | (d << 24),
            (b & low) | ((d >> 8) << 24),
            (c & low) | ((d >> 16) << 24),
        ],
        axis=0,
    )


def iota(shape, axis):
    return lax.broadcasted_iota(jnp.int32, shape, axis)


def dot(a, b, axes=((1,), (0,))):
    return lax.dot_general(a, b, (axes, ((), ())), preferred_element_type=F32)


def early_kernel(steps, rows, stored, size, *refs):
    @pl.when(lax.axis_index("tensor") < size // 2)
    def _():
        route(steps, rows, stored, *refs)


def late_kernel(steps, rows, stored, size, *refs):
    held, made = refs[3:5], refs[5:]

    @pl.when(lax.axis_index("tensor") < size // 2)
    def _():
        for source, out in zip(held, made):
            out[...] = source[...]

    @pl.when(lax.axis_index("tensor") >= size // 2)
    def _():
        route(steps, rows, stored, *refs[:3], *made)


def route(steps, rows, stored, adapter_ref, storage_ref, x_ref, sent_ref, target_ref):
    tokens = steps * rows
    count = storage_ref.shape[1]
    groups = count // stored
    adapter = jnp.concatenate([adapter_ref[...]] * steps, axis=1)
    hits = jnp.where(iota((count, tokens), 0) == adapter, 1.0, 0.0).astype(BF16)
    storage = jnp.broadcast_to(storage_ref[...].astype(F32), (8, count)).astype(BF16)
    position = dot(storage, hits)[0:1]
    down = jnp.transpose(jnp.broadcast_to(position, (tokens, tokens))).astype(jnp.int32)
    position = position.astype(jnp.int32)
    owner = position // stored
    earlier = iota((rows, tokens), 0) < iota((rows, tokens), 1) % rows
    same = earlier & (down[:rows] // stored == owner)
    place = jnp.sum(jnp.where(same, 1.0, 0.0), axis=0, keepdims=True).astype(jnp.int32)
    lane = iota((1, tokens), 1)
    target = owner * SLOT_ROWS + place * steps + lane // rows
    noted = jnp.where((place == 0) & (lane < rows), owner * SLOT_ROWS + MOST_ROWS * steps, -1)
    at = iota((groups * SLOT_ROWS, tokens), 0)
    pick = jnp.concatenate(
        [jnp.where(at == t, 1.0, 0.0).astype(BF16) for t in (target, noted)], axis=1
    )
    slot = (down % stored).astype(F32).astype(BF16)
    slot = jnp.concatenate([slot] * (x_ref.shape[1] // tokens), axis=1)
    sent_ref[...] = dot(pick, jnp.concatenate([x_ref[...], slot], axis=0)).astype(BF16)
    target_ref[...] = jnp.broadcast_to(target, target_ref.shape)


def turn_kernel(up_ref, target_ref, out_ref, turned_ref):
    stored, cols, ranks = up_ref.shape
    for a in range(stored):
        turned = jnp.transpose(up_ref[a].astype(F32)).astype(BF16)
        out_ref[a] = jnp.concatenate([turned[: ranks // 2], turned[ranks // 2 :]], axis=1)
    tokens = target_ref.shape[1]
    target = jnp.broadcast_to(target_ref[0:1].astype(F32), (tokens, tokens))
    turned_ref[...] = jnp.transpose(target).astype(jnp.int32)


def owner_kernel(note_row, taken_ref, down_ref, up_ref, back_ref):
    stored, _, ranks = down_ref.shape
    groups = back_ref.shape[0]
    up_rows = up_ref.shape[1]
    taken = taken_ref[...]
    slot = taken.reshape(groups, SLOT_ROWS, -1)[:, note_row : note_row + 1, 0:1].astype(F32)
    for a in range(0, stored, 2):
        pair = dot(taken, jnp.concatenate([down_ref[a], down_ref[a + 1]], axis=1))
        for i in range(2):
            y = pair[:, i * ranks : (i + 1) * ranks].reshape(groups, SLOT_ROWS, ranks)
            lowered = y if a + i == 0 else jnp.where(slot == a + i, y, lowered)
    back_ref[:, up_rows:, :] = lowered.astype(BF16)
    maps = [up_ref[a] for a in range(stored)]
    shape = maps[0].shape
    for g in range(groups):
        mine = jnp.broadcast_to(slot[g].astype(BF16), shape)
        chosen = maps[0]
        for a in range(1, stored):
            chosen = jnp.where(mine == jnp.full(shape, a, BF16), maps[a], chosen)
        back_ref[g, :up_rows, :] = chosen


def scale_kernel(x_ref, out_ref):
    out_ref[...] = (x_ref[...].astype(F32) * X_SCALE).astype(BF16)


def rows_kernel(back_ref, target_ref, x_ref, both_ref):
    groups, _, ranks = back_ref.shape
    tokens = target_ref.shape[0]
    held = back_ref[:, -SLOT_ROWS:, :].reshape(groups * SLOT_ROWS, ranks)
    target = target_ref[...]
    pick = jnp.concatenate(
        [
            jnp.where(iota((tokens, tokens), 1) + b * tokens == target, 1.0, 0.0).astype(BF16)
            for b in range(groups * SLOT_ROWS // tokens)
        ],
        axis=1,
    )
    width = x_ref.shape[1]
    both_ref[:, :width] = x_ref[...]
    both_ref[:, width:] = (dot(pick, held) * PART_SCALE).astype(BF16)


def delta_kernel(both_ref, back_ref, target_ref, out_ref):
    devices, tokens, _ = both_ref.shape
    groups, _, ranks = back_ref.shape
    width = both_ref.shape[2] - ranks
    half = ranks // 2
    shrink = both_ref[0, :, width:].astype(F32)
    for t in range(1, devices):
        shrink = shrink + both_ref[t, :, width:].astype(F32)
    shrink = shrink * (1.0 / PART_SCALE)
    owner = target_ref[...] // SLOT_ROWS
    lane = iota((half, ranks), 1)
    out_ref[...] = jnp.zeros_like(out_ref)
    for o in range(0, groups, 2):
        left, right = [], []
        for i in (o, o + 1):
            left.append(jnp.where(owner == i, shrink, 0.0).astype(BF16))
            up = back_ref[i, :half, :].astype(F32)
            right.append(jnp.where(lane < half, up, 0.0).astype(BF16))
            right.append(jnp.where(lane < half, 0.0, up).astype(BF16))
        out_ref[...] += dot(jnp.concatenate(left, axis=1), jnp.concatenate(right, axis=0))


def new_kernel(both_ref, delta_ref, w_ref, key_ref, value_ref, total):
    cols = key_ref.shape[1]
    devices = both_ref.shape[0]
    width = w_ref.shape[1] // devices
    total[...] = delta_ref[...] * X_SCALE
    for t in range(devices):
        total[...] += dot(
            both_ref[t, :, :width], w_ref[:, t * width : (t + 1) * width], ((1,), (1,))
        )
    new = (total[...] * (1.0 / X_SCALE)).astype(BF16)
    key_ref[...] = new[:, :cols]
    value_ref[...] = new[:, cols:]


def whole_kernel(lengths_ref, words_ref, scores_ref, _, out_ref):
    rows, queries, positions = scores_ref.shape
    quarter = rows // 4
    inside = iota((queries, positions), 1)
    for i in range(quarter):
        a, b, c = (words_ref[i + k * quarter] for k in range(3))
        d = ((a >> 24) & 255) | (((b >> 24) & 255) << 8) | ((c >> 24) << 16)
        for k, steps in enumerate(((a << 8) >> 8, (b << 8) >> 8, (c << 8) >> 8, d)):
            r = i + k * quarter
            score = scores_ref[r] + steps.astype(F32) * 2.0**-11
            out_ref[r] = jnp.where(inside < lengths_ref[r], score, -jnp.inf)


def local(
    normed_inputs,
    queries,
    key_value_weight,
    adapter_down_maps,
    adapter_up_maps,
    stored_key_rows,
    stored_value_rows,
    request_adapter,
    lengths,
    adapter_storage,
):
    steps, rows, width = normed_inputs.shape
    tokens = steps * rows
    stored, _, ranks = adapter_down_maps.shape
    cols = key_value_weight.shape[1]
    positions = stored_key_rows.shape[2]
    groups = lax.axis_size("batch")
    devices = lax.axis_size("tensor")
    members = width // cols
    rank = ranks // 2
    full = key_value_weight.shape[2]
    params = pltpu.CompilerParams(vmem_limit_bytes=32 * 2**20)

    x = normed_inputs.reshape(tokens, width)

    scale = 1.0 / math.sqrt(HD)
    query = jnp.transpose(queries.reshape(steps, rows, members, cols), (1, 0, 2, 3))
    query = query.reshape(rows, steps * members, cols)
    scores = scale * jnp.einsum(
        "rme,ret->rmt", query, stored_key_rows, preferred_element_type=F32
    )
    plan = (request_adapter.reshape(1, -1), adapter_storage.reshape(1, -1), x)
    routed = (
        jax.ShapeDtypeStruct((groups * SLOT_ROWS, width), BF16),
        jax.ShapeDtypeStruct((8, tokens), jnp.int32),
    )
    early = pl.pallas_call(
        functools.partial(early_kernel, steps, rows, stored, devices),
        out_shape=routed,
        in_specs=[VMEM] * 3,
        out_specs=(VMEM, VMEM),
        compiler_params=params,
        name="early",
    )(*plan)
    packed, *early = lax.optimization_barrier((pack(scores), *early))
    words = partner(packed)
    sent, target = pl.pallas_call(
        functools.partial(late_kernel, steps, rows, stored, devices),
        out_shape=routed,
        in_specs=[VMEM] * 5,
        out_specs=(VMEM, VMEM),
        compiler_params=params,
        name="route",
    )(*plan, *early)
    taken = lax.all_to_all(
        sent.reshape(groups, SLOT_ROWS, width), "batch", 0, 0, tiled=True
    ).reshape(groups * SLOT_ROWS, width)
    up, target = pl.pallas_call(
        turn_kernel,
        out_shape=(
            jax.ShapeDtypeStruct((stored, rank, 2 * cols), BF16),
            jax.ShapeDtypeStruct((tokens, tokens), jnp.int32),
        ),
        in_specs=[VMEM] * 2,
        out_specs=(VMEM, VMEM),
        compiler_params=params,
        cost_estimate=pl.CostEstimate(flops=TURN_FLOPS, bytes_accessed=2**18, transcendentals=0),
        name="turn",
    )(adapter_up_maps, target)
    back = pl.pallas_call(
        functools.partial(owner_kernel, MOST_ROWS * steps),
        out_shape=jax.ShapeDtypeStruct((groups, rank + SLOT_ROWS, ranks), BF16),
        in_specs=[VMEM] * 3,
        out_specs=VMEM,
        compiler_params=params,
        name="owner",
    )(taken, adapter_down_maps, up)
    back = lax.all_to_all(back, "batch", 0, 0, tiled=True)
    scaled = pl.pallas_call(
        scale_kernel,
        out_shape=jax.ShapeDtypeStruct(x.shape, BF16),
        in_specs=[VMEM],
        out_specs=VMEM,
        compiler_params=params,
        cost_estimate=pl.CostEstimate(flops=TURN_FLOPS, bytes_accessed=2**18, transcendentals=0),
        name="scale",
    )(x)
    both = pl.pallas_call(
        rows_kernel,
        out_shape=jax.ShapeDtypeStruct((tokens, width + ranks), BF16),
        in_specs=[VMEM] * 3,
        out_specs=VMEM,
        compiler_params=params,
        name="rows",
    )(back, target, scaled)
    both = lax.all_gather(both.astype(F16), "tensor", axis=0, tiled=False).astype(BF16)
    delta = pl.pallas_call(
        delta_kernel,
        out_shape=jax.ShapeDtypeStruct((tokens, 2 * cols), F32),
        in_specs=[VMEM] * 3,
        out_specs=VMEM,
        compiler_params=params,
        name="delta",
    )(both, back, target)
    new_shape = jax.ShapeDtypeStruct((tokens, cols), BF16)
    fresh_keys, fresh_values = pl.pallas_call(
        new_kernel,
        out_shape=(new_shape, new_shape),
        in_specs=[VMEM] * 3,
        out_specs=(VMEM, VMEM),
        scratch_shapes=[pltpu.VMEM((tokens, 2 * cols), F32)],
        compiler_params=params,
        name="new_kv",
    )(both, delta, key_value_weight.reshape(2 * cols, full))
    fresh_keys = fresh_keys.reshape(steps, rows, cols)
    fresh_values = fresh_values.reshape(steps, rows, cols)

    fresh = jnp.einsum("rme,jre->rjm", query, fresh_keys, preferred_element_type=F32)
    fresh = fresh.reshape(rows, -1)
    scores = pl.pallas_call(
        whole_kernel,
        out_shape=jax.ShapeDtypeStruct(scores.shape, F32),
        in_specs=[SMEM, VMEM, VMEM, HBM],
        out_specs=VMEM,
        compiler_params=params,
        name="whole",
    )(lengths, words, scores, fresh)
    peak = jnp.max(scores, axis=-1)
    risen = jnp.exp(scores - peak[:, :, None])
    mass = jnp.sum(risen, axis=-1)
    cached = jnp.einsum(
        "rmt,ret->rme", risen.astype(BF16), stored_value_rows, preferred_element_type=F32
    )
    cached, peak, mass = lax.optimization_barrier((cached, peak, mass))
    fresh = (fresh + partner(fresh)).reshape(rows, steps, -1)
    step_of = jnp.arange(steps * members) // members
    causal = (jnp.arange(steps)[:, None] <= step_of[None, :])[None]
    fresh = jnp.where(causal, fresh * scale, -jnp.inf)
    highest = jnp.maximum(peak, jnp.max(fresh, axis=1))
    fresh_exp = jnp.exp(fresh - highest[:, None, :])
    fall = jnp.exp(peak - highest)
    sums = mass * fall + jnp.sum(fresh_exp, axis=1)
    fresh_weights = (fresh_exp / sums[:, None, :]).astype(BF16)
    mixed = cached * (fall / sums)[:, :, None] + jnp.einsum(
        "rjm,jre->rme", fresh_weights, fresh_values, preferred_element_type=F32
    )
    mixed = mixed.astype(BF16).reshape(rows, steps, members * cols)
    return jnp.transpose(mixed, (1, 0, 2))


def solution(mesh):
    return jax.shard_map(
        local,
        mesh=mesh,
        in_specs=(
            P(None, "batch", "tensor"),
            P(None, "batch", "tensor"),
            P(None, "tensor", None),
            P("batch", "tensor", None),
            P("batch", "tensor", None),
            P("batch", "tensor", None),
            P("batch", "tensor", None),
            P("batch"),
            P("batch"),
            P(),
        ),
        out_specs=P(None, "batch", "tensor"),
        check_vma=False,
    )
```

```python
import functools
import math

import jax
import jax.numpy as jnp
from jax import lax
from jax.experimental import pallas as pl
from jax.experimental.pallas import tpu as pltpu
from jax.sharding import PartitionSpec as P

HD = 128
MOST_ROWS = 3
SLOT_ROWS = 16
BF16 = jnp.bfloat16
F16 = jnp.float16
F32 = jnp.float32
X_SCALE = 2.0**12
PART_SCALE = 2.0**8
TURN_FLOPS = 2**36
VMEM = pl.BlockSpec(memory_space=pltpu.VMEM)
SMEM = pl.BlockSpec(memory_space=pltpu.SMEM)
HBM = pl.BlockSpec(memory_space=pltpu.HBM)


def partner(value):
    size = lax.axis_size("tensor")
    return lax.ppermute(value, "tensor", [(i, i ^ (size // 2)) for i in range(size)])


def pack(scores):
    steps = jnp.clip(jnp.round(scores * 2.0**11), -(2.0**23), 2.0**23 - 1).astype(jnp.int32)
    a, b, c, d = jnp.split(steps, 4, axis=0)
    low = 2**24 - 1
    return jnp.concatenate(
        [
            (a & low) | (d << 24),
            (b & low) | ((d >> 8) << 24),
            (c & low) | ((d >> 16) << 24),
        ],
        axis=0,
    )


def iota(shape, axis):
    return lax.broadcasted_iota(jnp.int32, shape, axis)


def dot(a, b, axes=((1,), (0,))):
    return lax.dot_general(a, b, (axes, ((), ())), preferred_element_type=F32)


def early_kernel(steps, rows, stored, size, *refs):
    @pl.when(lax.axis_index("tensor") < size // 2)
    def _():
        route(steps, rows, stored, *refs)


def late_kernel(steps, rows, stored, size, *refs):
    held, made = refs[3:5], refs[5:]

    @pl.when(lax.axis_index("tensor") < size // 2)
    def _():
        for source, out in zip(held, made):
            out[...] = source[...]

    @pl.when(lax.axis_index("tensor") >= size // 2)
    def _():
        route(steps, rows, stored, *refs[:3], *made)


def route(steps, rows, stored, adapter_ref, storage_ref, x_ref, sent_ref, target_ref):
    tokens = steps * rows
    count = storage_ref.shape[1]
    groups = count // stored
    adapter = jnp.concatenate([adapter_ref[...]] * steps, axis=1)
    hits = jnp.where(iota((count, tokens), 0) == adapter, 1.0, 0.0).astype(BF16)
    storage = jnp.broadcast_to(storage_ref[...].astype(F32), (8, count)).astype(BF16)
    position = dot(storage, hits)[0:1]
    down = jnp.transpose(jnp.broadcast_to(position, (tokens, tokens))).astype(jnp.int32)
    position = position.astype(jnp.int32)
    owner = position // stored
    earlier = iota((rows, tokens), 0) < iota((rows, tokens), 1) % rows
    same = earlier & (down[:rows] // stored == owner)
    place = jnp.sum(jnp.where(same, 1.0, 0.0), axis=0, keepdims=True).astype(jnp.int32)
    lane = iota((1, tokens), 1)
    target = owner * SLOT_ROWS + place * steps + lane // rows
    noted = jnp.where((place == 0) & (lane < rows), owner * SLOT_ROWS + MOST_ROWS * steps, -1)
    at = iota((groups * SLOT_ROWS, tokens), 0)
    pick = jnp.concatenate(
        [jnp.where(at == t, 1.0, 0.0).astype(BF16) for t in (target, noted)], axis=1
    )
    slot = (down % stored).astype(F32).astype(BF16)
    slot = jnp.concatenate([slot] * (x_ref.shape[1] // tokens), axis=1)
    sent_ref[...] = dot(pick, jnp.concatenate([x_ref[...], slot], axis=0)).astype(BF16)
    target_ref[...] = jnp.broadcast_to(target, target_ref.shape)


def turn_kernel(up_ref, target_ref, out_ref, turned_ref):
    stored, cols, ranks = up_ref.shape
    for a in range(stored):
        turned = jnp.transpose(up_ref[a].astype(F32)).astype(BF16)
        out_ref[a] = jnp.concatenate([turned[: ranks // 2], turned[ranks // 2 :]], axis=1)
    tokens = target_ref.shape[1]
    target = jnp.broadcast_to(target_ref[0:1].astype(F32), (tokens, tokens))
    turned_ref[...] = jnp.transpose(target).astype(jnp.int32)


def owner_kernel(note_row, taken_ref, down_ref, up_ref, back_ref):
    stored, _, ranks = down_ref.shape
    groups = back_ref.shape[0]
    up_rows = up_ref.shape[1]
    taken = taken_ref[...]
    slot = taken.reshape(groups, SLOT_ROWS, -1)[:, note_row : note_row + 1, 0:1].astype(F32)
    maps = [up_ref[a] for a in range(stored)]
    shape = maps[0].shape
    share = groups // (stored // 2)
    for a in range(0, stored, 2):
        pair = dot(taken, jnp.concatenate([down_ref[a], down_ref[a + 1]], axis=1))
        for g in range(a // 2 * share, (a // 2 + 1) * share):
            mine = jnp.broadcast_to(slot[g].astype(BF16), shape)
            chosen = maps[0]
            for i in range(1, stored):
                chosen = jnp.where(mine == jnp.full(shape, i, BF16), maps[i], chosen)
            back_ref[g, :up_rows, :] = chosen
        for i in range(2):
            y = pair[:, i * ranks : (i + 1) * ranks].reshape(groups, SLOT_ROWS, ranks)
            lowered = y if a + i == 0 else jnp.where(slot == a + i, y, lowered)
    back_ref[:, up_rows:, :] = lowered.astype(BF16)


def scale_kernel(x_ref, out_ref):
    out_ref[...] = (x_ref[...].astype(F32) * X_SCALE).astype(BF16)


def rows_kernel(back_ref, target_ref, x_ref, both_ref):
    groups, _, ranks = back_ref.shape
    tokens = target_ref.shape[0]
    held = back_ref[:, -SLOT_ROWS:, :].reshape(groups * SLOT_ROWS, ranks)
    target = target_ref[...]
    pick = jnp.concatenate(
        [
            jnp.where(iota((tokens, tokens), 1) + b * tokens == target, 1.0, 0.0).astype(BF16)
            for b in range(groups * SLOT_ROWS // tokens)
        ],
        axis=1,
    )
    width = x_ref.shape[1]
    both_ref[:, :width] = x_ref[...]
    both_ref[:, width:] = (dot(pick, held) * PART_SCALE).astype(BF16)


def delta_kernel(both_ref, back_ref, target_ref, out_ref):
    devices, tokens, _ = both_ref.shape
    groups, _, ranks = back_ref.shape
    width = both_ref.shape[2] - ranks
    half = ranks // 2
    shrink = both_ref[0, :, width:].astype(F32)
    for t in range(1, devices):
        shrink = shrink + both_ref[t, :, width:].astype(F32)
    shrink = shrink * (1.0 / PART_SCALE)
    owner = target_ref[...] // SLOT_ROWS
    lane = iota((half, ranks), 1)
    out_ref[...] = jnp.zeros_like(out_ref)
    for o in range(0, groups, 2):
        left, right = [], []
        for i in (o, o + 1):
            left.append(jnp.where(owner == i, shrink, 0.0).astype(BF16))
            up = back_ref[i, :half, :].astype(F32)
            right.append(jnp.where(lane < half, up, 0.0).astype(BF16))
            right.append(jnp.where(lane < half, 0.0, up).astype(BF16))
        out_ref[...] += dot(jnp.concatenate(left, axis=1), jnp.concatenate(right, axis=0))


def new_kernel(both_ref, delta_ref, w_ref, key_ref, value_ref, total):
    cols = key_ref.shape[1]
    devices = both_ref.shape[0]
    width = w_ref.shape[1] // devices
    total[...] = delta_ref[...] * X_SCALE
    for t in range(devices):
        total[...] += dot(
            both_ref[t, :, :width], w_ref[:, t * width : (t + 1) * width], ((1,), (1,))
        )
    new = (total[...] * (1.0 / X_SCALE)).astype(BF16)
    key_ref[...] = new[:, :cols]
    value_ref[...] = new[:, cols:]


def whole_kernel(lengths_ref, words_ref, scores_ref, _, out_ref):
    rows, queries, positions = scores_ref.shape
    quarter = rows // 4
    inside = iota((queries, positions), 1)
    for i in range(quarter):
        a, b, c = (words_ref[i + k * quarter] for k in range(3))
        d = ((a >> 24) & 255) | (((b >> 24) & 255) << 8) | ((c >> 24) << 16)
        for k, steps in enumerate(((a << 8) >> 8, (b << 8) >> 8, (c << 8) >> 8, d)):
            r = i + k * quarter
            score = scores_ref[r] + steps.astype(F32) * 2.0**-11
            out_ref[r] = jnp.where(inside < lengths_ref[r], score, -jnp.inf)


def local(
    normed_inputs,
    queries,
    key_value_weight,
    adapter_down_maps,
    adapter_up_maps,
    stored_key_rows,
    stored_value_rows,
    request_adapter,
    lengths,
    adapter_storage,
):
    steps, rows, width = normed_inputs.shape
    tokens = steps * rows
    stored, _, ranks = adapter_down_maps.shape
    cols = key_value_weight.shape[1]
    positions = stored_key_rows.shape[2]
    groups = lax.axis_size("batch")
    devices = lax.axis_size("tensor")
    members = width // cols
    rank = ranks // 2
    full = key_value_weight.shape[2]
    params = pltpu.CompilerParams(vmem_limit_bytes=32 * 2**20)

    x = normed_inputs.reshape(tokens, width)

    scale = 1.0 / math.sqrt(HD)
    query = jnp.transpose(queries.reshape(steps, rows, members, cols), (1, 0, 2, 3))
    query = query.reshape(rows, steps * members, cols)
    scores = scale * jnp.einsum(
        "rme,ret->rmt", query, stored_key_rows, preferred_element_type=F32
    )
    plan = (request_adapter.reshape(1, -1), adapter_storage.reshape(1, -1), x)
    routed = (
        jax.ShapeDtypeStruct((groups * SLOT_ROWS, width), BF16),
        jax.ShapeDtypeStruct((8, tokens), jnp.int32),
    )
    early = pl.pallas_call(
        functools.partial(early_kernel, steps, rows, stored, devices),
        out_shape=routed,
        in_specs=[VMEM] * 3,
        out_specs=(VMEM, VMEM),
        compiler_params=params,
        name="early",
    )(*plan)
    packed, *early = lax.optimization_barrier((pack(scores), *early))
    words = partner(packed)
    sent, target = pl.pallas_call(
        functools.partial(late_kernel, steps, rows, stored, devices),
        out_shape=routed,
        in_specs=[VMEM] * 5,
        out_specs=(VMEM, VMEM),
        compiler_params=params,
        name="route",
    )(*plan, *early)
    taken = lax.all_to_all(
        sent.reshape(groups, SLOT_ROWS, width), "batch", 0, 0, tiled=True
    ).reshape(groups * SLOT_ROWS, width)
    up, target = pl.pallas_call(
        turn_kernel,
        out_shape=(
            jax.ShapeDtypeStruct((stored, rank, 2 * cols), BF16),
            jax.ShapeDtypeStruct((tokens, tokens), jnp.int32),
        ),
        in_specs=[VMEM] * 2,
        out_specs=(VMEM, VMEM),
        compiler_params=params,
        cost_estimate=pl.CostEstimate(flops=TURN_FLOPS, bytes_accessed=2**18, transcendentals=0),
        name="turn",
    )(adapter_up_maps, target)
    back = pl.pallas_call(
        functools.partial(owner_kernel, MOST_ROWS * steps),
        out_shape=jax.ShapeDtypeStruct((groups, rank + SLOT_ROWS, ranks), BF16),
        in_specs=[VMEM] * 3,
        out_specs=VMEM,
        compiler_params=params,
        name="owner",
    )(taken, adapter_down_maps, up)
    back = lax.all_to_all(back, "batch", 0, 0, tiled=True)
    scaled = pl.pallas_call(
        scale_kernel,
        out_shape=jax.ShapeDtypeStruct(x.shape, BF16),
        in_specs=[VMEM],
        out_specs=VMEM,
        compiler_params=params,
        cost_estimate=pl.CostEstimate(flops=TURN_FLOPS, bytes_accessed=2**18, transcendentals=0),
        name="scale",
    )(x)
    both = pl.pallas_call(
        rows_kernel,
        out_shape=jax.ShapeDtypeStruct((tokens, width + ranks), BF16),
        in_specs=[VMEM] * 3,
        out_specs=VMEM,
        compiler_params=params,
        name="rows",
    )(back, target, scaled)
    both = lax.all_gather(both.astype(F16), "tensor", axis=0, tiled=False).astype(BF16)
    delta = pl.pallas_call(
        delta_kernel,
        out_shape=jax.ShapeDtypeStruct((tokens, 2 * cols), F32),
        in_specs=[VMEM] * 3,
        out_specs=VMEM,
        compiler_params=params,
        name="delta",
    )(both, back, target)
    new_shape = jax.ShapeDtypeStruct((tokens, cols), BF16)
    fresh_keys, fresh_values = pl.pallas_call(
        new_kernel,
        out_shape=(new_shape, new_shape),
        in_specs=[VMEM] * 3,
        out_specs=(VMEM, VMEM),
        scratch_shapes=[pltpu.VMEM((tokens, 2 * cols), F32)],
        compiler_params=params,
        name="new_kv",
    )(both, delta, key_value_weight.reshape(2 * cols, full))
    fresh_keys = fresh_keys.reshape(steps, rows, cols)
    fresh_values = fresh_values.reshape(steps, rows, cols)

    fresh = jnp.einsum("rme,jre->rjm", query, fresh_keys, preferred_element_type=F32)
    fresh = fresh.reshape(rows, -1)
    scores = pl.pallas_call(
        whole_kernel,
        out_shape=jax.ShapeDtypeStruct(scores.shape, F32),
        in_specs=[SMEM, VMEM, VMEM, HBM],
        out_specs=VMEM,
        compiler_params=params,
        name="whole",
    )(lengths, words, scores, fresh)
    peak = jnp.max(scores, axis=-1)
    risen = jnp.exp(scores - peak[:, :, None])
    mass = jnp.sum(risen, axis=-1)
    cached = jnp.einsum(
        "rmt,ret->rme", risen.astype(BF16), stored_value_rows, preferred_element_type=F32
    )
    cached, peak, mass = lax.optimization_barrier((cached, peak, mass))
    fresh = (fresh + partner(fresh)).reshape(rows, steps, -1)
    step_of = jnp.arange(steps * members) // members
    causal = (jnp.arange(steps)[:, None] <= step_of[None, :])[None]
    fresh = jnp.where(causal, fresh * scale, -jnp.inf)
    highest = jnp.maximum(peak, jnp.max(fresh, axis=1))
    fresh_exp = jnp.exp(fresh - highest[:, None, :])
    fall = jnp.exp(peak - highest)
    sums = mass * fall + jnp.sum(fresh_exp, axis=1)
    fresh_weights = (fresh_exp / sums[:, None, :]).astype(BF16)
    mixed = cached * (fall / sums)[:, :, None] + jnp.einsum(
        "rjm,jre->rme", fresh_weights, fresh_values, preferred_element_type=F32
    )
    mixed = mixed.astype(BF16).reshape(rows, steps, members * cols)
    return jnp.transpose(mixed, (1, 0, 2))


def solution(mesh):
    return jax.shard_map(
        local,
        mesh=mesh,
        in_specs=(
            P(None, "batch", "tensor"),
            P(None, "batch", "tensor"),
            P(None, "tensor", None),
            P("batch", "tensor", None),
            P("batch", "tensor", None),
            P("batch", "tensor", None),
            P("batch", "tensor", None),
            P("batch"),
            P("batch"),
            P(),
        ),
        out_specs=P(None, "batch", "tensor"),
        check_vma=False,
    )
```
